128 devices in a mesh: dp: 32 (over y, x, z_lo), tensor: 4 (over z_hi, core).
Axes of the slice: x: 4, y: 4, z: 4 (z_hi: 2, z_lo: 2; z = z_hi * 2 + z_lo), core: 2. Of those that a mesh axis runs over, the one named last changes fastest.
Arguments:
- activations: bfloat16 [2, 65536, 4096], P(None, 'dp', 'tensor'), may hold values from -6 to 6
- out_grads: bfloat16 [2, 65536, 4096], P(None, 'dp', 'tensor'), may hold values from -6 to 6
- proj_in: bfloat16 [2, 4096, 16], P(None, 'tensor'), may hold values from -0.09375 to 0.09375
- proj_out: bfloat16 [2, 4096, 16], P(None, 'tensor'), may hold values from -0.09375 to 0.09375
- lengths: int32 [1024], P('dp'), may hold values from 16 to 64
- queries: float32 [512, 512], P('dp', 'tensor'), may hold values from -6 to 6
Outputs:
- scores: float32 [1024, 512], P('dp', 'tensor')
The draws below stay inside these ranges and needn't reach their ends.
All inputs are finite; a program needn't handle non-finite values.
Results may differ from the reference program's by a relative error of at most 0.028.
Values may be sent and summed in bfloat16 or wider, within the bound.
A program may use at most 64 MiB of HBM per device.

```python
import math
import jax
import jax.numpy as jnp
from jax import lax

D = 4096
R = 16
LIN = 2
LEN = 64
ITERS = 4
K = 512
SEQS = 1024
TOKENS = 65536
Q = 512


def place_ends(drawn, stream_key, low, top_value):
    place = [jax.random.randint(jax.random.fold_in(stream_key, axis), (), 0, length) for axis, length in enumerate(drawn.shape)]
    widest = drawn.shape.index(max(drawn.shape))
    neighbour = place[:widest] + [(place[widest] + 1) % drawn.shape[widest]] + place[widest + 1:]
    return drawn.at[tuple(place)].set(low).at[tuple(neighbour)].set(top_value)


def steps_of(own_key, shape, pieces, least, largest):
    level = 1.0
    for dim, blocks in pieces:
        draws = jax.random.uniform(jax.random.fold_in(jax.random.fold_in(own_key, 6), dim), (blocks,), jnp.float32, least / len(pieces), largest / len(pieces))
        level = level * jnp.repeat(jnp.exp(draws), shape[dim] // blocks).reshape((-1,) + (1,) * (len(shape) - 1 - dim))
    return level


def bell_draw(key, dims, width, bound, cuts=(), kind=jnp.bfloat16):
    factor_of = steps_of(key, dims, cuts, -0.22, 0.18) if cuts else 1.0
    values = jax.random.normal(key, dims, jnp.float32) * width * factor_of
    return jnp.minimum(jnp.maximum(values, -bound), bound).astype(kind)


def setup_inputs(seed: int = 0) -> dict:
    key_of = jax.random.split(jax.random.key(seed), 7)
    activations = bell_draw(key_of[0], (LIN, TOKENS, D), 1.0, 6.0, ((1, 32), (2, 4)))
    out_grads = bell_draw(key_of[1], (LIN, TOKENS, D), 1.0, 6.0, ((1, 32), (2, 4)))
    proj_in = bell_draw(key_of[2], (LIN, D, R), D ** -0.5, 0.09375, ((1, 4),))
    proj_out = bell_draw(key_of[3], (LIN, D, R), D ** -0.5, 0.09375, ((1, 4),))
    lengths = place_ends(jax.random.randint(key_of[4], (SEQS,), LEN // 4, LEN + 1), jax.random.fold_in(key_of[4], 1), LEN // 4, LEN).astype(jnp.int32)
    queries = bell_draw(key_of[5], (K, Q), 1.0, 6.0, ((0, 32), (1, 4)), jnp.float32)
    return {"activations": activations, "out_grads": out_grads, "proj_in": proj_in, "proj_out": proj_out, "lengths": lengths, "queries": queries}


DAMPING = 0.1

def project(activations, out_grads, proj_in, proj_out, lengths):
    live_tokens = (jnp.arange(LEN)[None, :] < lengths[:, None]).astype(jnp.float32)
    columns = []
    for linear in range(LIN):
        inner_proj = jnp.dot(activations[linear], proj_in[linear], preferred_element_type=jnp.float32).reshape(SEQS, LEN, R)
        outer_proj = jnp.dot(out_grads[linear], proj_out[linear], preferred_element_type=jnp.float32).reshape(SEQS, LEN, R)
        seq_blocks = jnp.einsum('sta,stb->sab', outer_proj * live_tokens[:, :, None], inner_proj) / math.sqrt(LEN)
        columns.append(seq_blocks.reshape(SEQS, R * R))
    return jnp.concatenate(columns, axis=1).astype(jnp.bfloat16)

def reference(activations, out_grads, proj_in, proj_out, lengths, queries):
    vectors = project(activations, out_grads, proj_in, proj_out, lengths)
    gram_all = jnp.dot(vectors.T, vectors, preferred_element_type=jnp.float32) / SEQS

    def apply_operator(direction):
        return jnp.dot(gram_all, direction, precision=lax.Precision.HIGHEST, preferred_element_type=jnp.float32) + DAMPING * direction
    solution = jnp.zeros_like(queries)
    residual = queries
    direction = queries
    norm_now = lax.optimization_barrier(jnp.sum(residual * residual, axis=0))
    for iteration in range(ITERS):
        operator_image = apply_operator(direction)
        step_size = norm_now / lax.optimization_barrier(jnp.sum(direction * operator_image, axis=0))
        solution = solution + step_size * direction
        residual = residual - step_size * operator_image
        norm_next = lax.optimization_barrier(jnp.sum(residual * residual, axis=0))
        direction = residual + norm_next / norm_now * direction
        norm_now = norm_next
    solution_bf = solution.astype(jnp.bfloat16)
    return jnp.dot(vectors, solution_bf, preferred_element_type=jnp.float32) / math.sqrt(K)
```

```python
import functools
import math

import jax
import jax.numpy as jnp
from jax import lax
from jax.experimental import pallas as pl
from jax.experimental.pallas import tpu as pltpu
from jax.sharding import PartitionSpec as P

ITERS = 4
DAMPING = 0.1
MESH = pl.DeviceIdType.MESH
BF = jnp.bfloat16
F32 = jnp.float32

HOPS = lambda o: sum(min(v, 4 - v) for v in o)
OFFSETS = sorted(
    [(a, b, c) for a in range(4) for b in range(4) for c in range(4)], key=HOPS, reverse=True
)
SELF = len(OFFSETS) - 1
ACROSS = OFFSETS.index((0, 0, 2))
GROUPS = 4
PER_GROUP = len(OFFSETS) // GROUPS
SUB = 2


def split(v):
    hi = v.astype(BF)
    return hi, (v - hi.astype(F32)).astype(BF)


def tn_dot(a, b):
    return lax.dot_general(a, b, (((0,), (0,)), ((), ())), preferred_element_type=F32)


def kernel(
    act, grad, pin, pout, lengths, queries, out,
    abuf, gbuf, pbuf, w, send, part, vsend, own, oth, qbuf, lens, expand,
    in_sem, p_sem, q_sem, l_sem, rs_send, rs_recv, q_send, q_recv, v_send, v_recv, f_send, f_recv,
):
    dp, tensor = lax.axis_index("dp"), lax.axis_index("tensor")
    x, y = lax.rem(dp // 2, 4), dp // 8
    zh, core = tensor // 2, lax.rem(tensor, 2)
    z = zh * 2 + lax.rem(dp, 2)

    def chip(o, other=0):
        tx, ty, tz = (lax.rem(v + d, 4) for v, d in zip((x, y, z), o))
        tc = 1 - core if other else core
        return ((ty * 4 + tx) * 2 + lax.rem(tz, 2), (tz // 2) * 2 + tc)

    sibling = chip((0, 0, 0), 1)
    shares = ((0, 1), (1, 1), (1, 0), (0, 0))
    targets = (chip((0, 0, 2)), chip((0, 0, 2), 1), sibling)
    step = 1024 // SUB

    def load(k, s, which):
        rel, far = shares[k]
        linear = 1 - core if rel else core
        half = 1 - zh if far else zh
        src, dst = ((act, abuf), (grad, gbuf))[which]
        return pltpu.make_async_copy(
            src.at[linear, pl.ds(half * 1024 + s * step, step)],
            dst.at[k, pl.ds(s * step, step)],
            in_sem.at[k, s, which],
        )

    weights = [
        pltpu.make_async_copy(p.at[1 - core if rel else core], pbuf.at[io, rel], p_sem.at[io, rel])
        for io, p in enumerate((pin, pout)) for rel in range(2)
    ]
    for c in weights:
        c.start()
    for k in range(4):
        for s in range(SUB):
            for which in range(2):
                load(k, s, which).start()
    len_copy = pltpu.make_async_copy(lengths, lens, l_sem)
    len_copy.start()
    q_slot = lax.rem(dp + 16 * core, 32)
    q_copy = pltpu.make_async_copy(queries, qbuf.at[q_slot], q_sem)
    q_copy.start()

    barrier = pltpu.get_barrier_semaphore()
    for o in OFFSETS[:SELF]:
        pl.semaphore_signal(barrier, inc=1, device_id=chip(o), device_id_type=MESH)
    for t in targets[1:]:
        pl.semaphore_signal(barrier, inc=1, device_id=t, device_id_type=MESH)

    row = lax.rem(lax.broadcasted_iota(jnp.int32, (256, 256), 0), 128)
    col = lax.broadcasted_iota(jnp.int32, (256, 256), 1)
    for q in range(4):
        expand[q, 0] = jnp.where(row == 32 * q + lax.rem(col, 16), 1.0, 0.0).astype(BF)
        expand[q, 1] = jnp.where(row == 32 * q + 16 + col // 16, 1.0, 0.0).astype(BF)

    for c in weights:
        c.wait()
    zero = jnp.zeros((16, 1024), BF)
    for rel in range(2):
        w[0, rel] = jnp.concatenate([pbuf[0, rel], zero] * 4, axis=0).T
        w[1, rel] = jnp.concatenate([zero, pbuf[1, rel]] * 4, axis=0).T

    lane = lax.broadcasted_iota(jnp.int32, (256, 128), 1)
    token = lax.broadcasted_iota(jnp.int32, (256, 128), 0)
    quarter = lane // 32

    def project(k):
        rel = shares[k][0]
        total = None
        for q in range(4):
            if q % (4 // SUB) == 0:
                for which in range(2):
                    load(k, q // (4 // SUB), which).wait()
            rows = pl.ds(q * 256, 256)
            r = jnp.dot(abuf[k, rows], w[0, rel], preferred_element_type=F32)
            r = r + jnp.dot(gbuf[k, rows], w[1, rel], preferred_element_type=F32)
            total = r if total is None else jnp.where(quarter == q, r, total)
        return total

    def scatter(k):
        return pltpu.make_async_remote_copy(
            src_ref=send.at[k], dst_ref=part.at[k], send_sem=rs_send.at[k], recv_sem=rs_recv.at[k],
            device_id=targets[k], device_id_type=MESH,
        )

    def query_copy(o, low):
        tx, ty = lax.rem(x + o[0], 4), lax.rem(y + o[1], 4)
        tl = lax.rem(lax.rem(dp, 2) + low, 2)
        return pltpu.make_async_remote_copy(
            src_ref=queries, dst_ref=qbuf.at[q_slot], send_sem=q_send, recv_sem=q_recv,
            device_id=((ty * 4 + tx) * 2 + tl, tensor), device_id_type=MESH,
        )

    plane = [(a, b, l) for a in range(4) for b in range(4) for l in range(2) if a or b or l]

    send[0] = project(0).astype(BF)
    pl.semaphore_wait(barrier, SELF + 2)
    scatter(0).start()
    send[1] = project(1).astype(BF)
    scatter(1).start()
    for a, b, l in plane:
        query_copy((a, b), l).start()
    send[2] = project(2).astype(BF)
    scatter(2).start()
    total = project(3)

    len_copy.wait()
    blocks = []
    for rb in range(4):
        n = jnp.zeros((1, 128), jnp.int32)
        for q in range(4):
            n = jnp.where(quarter[:1] == q, lens[zh * 16 + 4 * q + rb], n)
        n = jnp.where(lax.rem(lane[:1], 32) < 16, 64, n)
        blocks.append(jnp.broadcast_to(n, (64, 128)))
    live = lax.rem(token, 64) < jnp.concatenate(blocks, axis=0)

    for k in (2, 0, 1):
        scatter(k).wait_recv()
        total = total + part[k].astype(F32)
    total = jnp.where(live, total, 0.0)
    both = jnp.concatenate(split(total), axis=1)
    rows = []
    for q in range(4):
        inner = jnp.dot(both, expand[q, 0], preferred_element_type=F32)
        outer = jnp.dot(both, expand[q, 1], preferred_element_type=F32)
        prod = outer * inner
        for rb in range(4):
            rows.append(jnp.sum(prod[rb * 64:(rb + 1) * 64], axis=0, keepdims=True))
    vec = (jnp.concatenate(rows, axis=0) * (1.0 / math.sqrt(64))).astype(BF)
    own[SELF] = vec

    def spread(k):
        return pltpu.make_async_remote_copy(
            src_ref=own.at[SELF], dst_ref=own.at[k], send_sem=v_send, recv_sem=v_recv.at[k // PER_GROUP],
            device_id=chip(OFFSETS[k]), device_id_type=MESH,
        )

    for k in range(SELF):
        spread(k).start()

    def group(g):
        return pl.ds(g * PER_GROUP, PER_GROUP)

    def forward(g):
        return pltpu.make_async_remote_copy(
            src_ref=own.at[group(g)], dst_ref=oth.at[group(g)], send_sem=f_send.at[g], recv_sem=f_recv.at[g],
            device_id=sibling, device_id_type=MESH,
        )

    for g in range(GROUPS):
        got = pl.ds(g * PER_GROUP, min(PER_GROUP, SELF - g * PER_GROUP))
        pltpu.make_async_copy(own.at[got], own.at[got], v_recv.at[g]).wait()
        forward(g).start()
    gram = jnp.zeros((512, 512), F32)
    for g in range(GROUPS):
        forward(g).wait_recv()
        vecs = jnp.concatenate(
            [own[group(g)].reshape(256, 256), oth[group(g)].reshape(256, 256)], axis=1
        )
        gram = gram + tn_dot(vecs, vecs)
    gram = gram * (1.0 / 1024)
    g_hi, g_lo = split(gram)

    q_copy.wait()
    others = pl.ds(0, 31)
    pltpu.make_async_copy(qbuf.at[others], qbuf.at[others], q_recv).wait()
    residual = qbuf[...].reshape(512, 128)
    direction = residual
    solution = jnp.zeros_like(residual)
    norm_now = jnp.sum(residual * residual, axis=0, keepdims=True)
    for it in range(ITERS):
        d_hi, d_lo = split(direction)
        wide = jnp.dot(g_hi, jnp.concatenate([d_hi, d_lo], axis=1), preferred_element_type=F32)
        image = wide[:, :128] + wide[:, 128:] + jnp.dot(g_lo, d_hi, preferred_element_type=F32)
        image = image + DAMPING * direction
        step_size = norm_now / jnp.sum(direction * image, axis=0, keepdims=True)
        solution = solution + step_size * direction
        if it < ITERS - 1:
            residual = residual - step_size * image
            norm_next = jnp.sum(residual * residual, axis=0, keepdims=True)
            direction = residual + norm_next / norm_now * direction
            norm_now = norm_next
    solution = solution.astype(BF)
    scale = 1.0 / math.sqrt(512)
    for slot, half in ((SELF, zh), (ACROSS, 1 - zh)):
        v = jnp.concatenate([own[slot], oth[slot]], axis=1)
        out[pl.ds(half * 16, 16)] = jnp.dot(v, solution, preferred_element_type=F32) * scale

    for k in range(3):
        scatter(k).wait_send()
    for g in range(GROUPS):
        forward(g).wait_send()
    pltpu.make_async_copy(own.at[pl.ds(0, SELF)], own.at[pl.ds(0, SELF)], v_send).wait()
    pltpu.make_async_copy(qbuf.at[others], qbuf.at[others], q_send).wait()


def on_device(activations, out_grads, proj_in, proj_out, lengths, queries):
    any_space = pl.BlockSpec(memory_space=pl.ANY)
    dma = pltpu.SemaphoreType.DMA
    vmem = pltpu.VMEM
    slots = len(OFFSETS)
    return pl.pallas_call(
        kernel,
        out_shape=jax.ShapeDtypeStruct((32, 128), F32),
        in_specs=[any_space] * 6,
        out_specs=pl.BlockSpec(memory_space=pltpu.VMEM),
        scratch_shapes=[
            vmem((4, 1024, 1024), BF),
            vmem((4, 1024, 1024), BF),
            vmem((2, 2, 16, 1024), BF),
            vmem((2, 2, 1024, 128), BF),
            vmem((3, 256, 128), BF),
            vmem((3, 256, 128), BF),
            vmem((16, 256), BF),
            vmem((slots, 16, 256), BF),
            vmem((slots, 16, 256), BF),
            vmem((32, 16, 128), F32),
            pltpu.SMEM((32,), jnp.int32),
            vmem((4, 2, 256, 256), BF),
            dma((4, SUB, 2)),
            dma((2, 2)),
            dma,
            dma,
            dma((3,)),
            dma((3,)),
            dma,
            dma,
            dma,
            dma((GROUPS,)),
            dma((GROUPS,)),
            dma((GROUPS,)),
        ],
        compiler_params=pltpu.CompilerParams(
            collective_id=0, has_side_effects=True, vmem_limit_bytes=48 << 20
        ),
        name="influence",
    )(
        activations, out_grads, jnp.swapaxes(proj_in, 1, 2), jnp.swapaxes(proj_out, 1, 2), lengths, queries
    )


def solution(mesh):
    placed = (
        P(None, "dp", "tensor"),
        P(None, "dp", "tensor"),
        P(None, "tensor", None),
        P(None, "tensor", None),
        P("dp"),
        P("dp", "tensor"),
    )
    return jax.shard_map(
        on_device, mesh=mesh, in_specs=placed, out_specs=P("dp", "tensor"), check_vma=False
    )
```

```python
import math

import jax
import jax.numpy as jnp
from jax import lax
from jax.experimental import pallas as pl
from jax.experimental.pallas import tpu as pltpu
from jax.sharding import PartitionSpec as P

ITERS = 4
DAMPING = 0.1
MESH = pl.DeviceIdType.MESH
BF = jnp.bfloat16
F32 = jnp.float32

OFFSETS = sorted(
    [(a, b, c) for a in range(4) for b in range(4) for c in range(4)],
    key=lambda o: -sum(min(v, 4 - v) for v in o),
)
SLOTS = len(OFFSETS)
SELF = SLOTS - 1
ACROSS = OFFSETS.index((0, 0, 2))
GROUPS = 4
PER_GROUP = SLOTS // GROUPS
SUB = 2


def split(v):
    hi = v.astype(BF)
    return hi, (v - hi.astype(F32)).astype(BF)


def nt_dot(a, b):
    return lax.dot_general(a, b, (((1,), (1,)), ((), ())), preferred_element_type=F32)


def tn_dot(a, b):
    return lax.dot_general(a, b, (((0,), (0,)), ((), ())), preferred_element_type=F32)


def kernel(
    act, grad, pin, pout, lengths, queries, out,
    abuf, gbuf, pbuf, send, part, acc, own, oth, qbuf, lens, p_hi, p_lo, gram, g_hi, sol, res, dirn, norm,
    in_sem, p_sem, q_sem, l_sem, rs_send, rs_recv, q_send, q_recv, v_send, v_recv, f_send, f_recv, plane_sem, all_sem,
):
    dp, tensor = lax.axis_index("dp"), lax.axis_index("tensor")
    x, y = lax.rem(dp // 2, 4), dp // 8
    zl = lax.rem(dp, 2)
    zh, core = tensor // 2, lax.rem(tensor, 2)
    z = zh * 2 + zl

    def chip(dx, dy, dz, flip=0):
        tx, ty, tz = lax.rem(x + dx, 4), lax.rem(y + dy, 4), lax.rem(z + dz, 4)
        return ((ty * 4 + tx) * 2 + lax.rem(tz, 2), (tz // 2) * 2 + lax.rem(core + flip, 2))

    sibling = chip(0, 0, 0, 1)
    step = 1024 // SUB

    def other_linear(k):
        return lax.rem((k + 1) // 2, 2)

    def far(k):
        return 1 - k // 2

    def load(k, s, which):
        linear = lax.rem(core + other_linear(k), 2)
        half = lax.rem(zh + far(k), 2)
        src, dst = ((act, abuf), (grad, gbuf))[which]
        return pltpu.make_async_copy(
            src.at[linear, pl.ds(pl.multiple_of(half * 1024 + s * step, step), step)],
            dst.at[k, pl.ds(pl.multiple_of(s * step, step), step)],
            in_sem.at[k, s, which],
        )

    def scatter(k):
        return pltpu.make_async_remote_copy(
            src_ref=send.at[k], dst_ref=part.at[k], send_sem=rs_send.at[k], recv_sem=rs_recv.at[k],
            device_id=chip(0, 0, 2 * far(k), other_linear(k)), device_id_type=MESH,
        )

    weights = [pltpu.make_async_copy(p, pbuf.at[io], p_sem.at[io]) for io, p in enumerate((pin, pout))]
    for c in weights:
        c.start()

    @pl.loop(0, 4 * SUB)
    def _(n):
        for which in range(2):
            load(n // SUB, lax.rem(n, SUB), which).start()

    len_copy = pltpu.make_async_copy(lengths, lens, l_sem)
    len_copy.start()
    q_y = lax.rem(y + 2 * core, 4)
    q_copy = pltpu.make_async_copy(queries, qbuf.at[q_y, zl, x], q_sem)
    q_copy.start()

    barrier = pltpu.get_barrier_semaphore()

    for t in (chip(0, 0, 2), chip(0, 0, 2, 1), sibling):
        pl.semaphore_signal(barrier, inc=1, device_id=t, device_id_type=MESH)
    for d in (1, 2, 3):
        for t in (chip(d, 0, 0), chip(0, d, 0)) + ((chip(0, 0, d),) if d != 2 else ()):
            pl.semaphore_signal(barrier, inc=1, device_id=t, device_id_type=MESH)

    def query_row(n):
        return pltpu.make_async_remote_copy(
            src_ref=qbuf.at[q_y, zl, x], dst_ref=qbuf.at[q_y, zl, x], send_sem=q_send.at[0], recv_sem=q_recv.at[0],
            device_id=chip(n, 0, 0), device_id_type=MESH,
        )

    def query_plane(n):
        ty, tl = lax.rem(y + lax.rem(n, 4), 4), lax.rem(zl + n // 4, 2)
        return pltpu.make_async_remote_copy(
            src_ref=qbuf.at[q_y, zl], dst_ref=qbuf.at[q_y, zl], send_sem=q_send.at[1], recv_sem=q_recv.at[1],
            device_id=((ty * 4 + x) * 2 + tl, tensor), device_id_type=MESH,
        )

    for c in weights:
        c.wait()

    @pl.loop(0, 4)
    def _(k):
        linear = lax.rem(core + other_linear(k), 2)

        for s in range(SUB):
            rows = pl.ds(s * step, step)
            for which, buf in enumerate((abuf, gbuf)):
                load(k, s, which).wait()
                acc[which * 16:which * 16 + 16, rows] = nt_dot(pbuf[which, linear], buf[k, rows])

        @pl.when(k == 0)
        def _():
            pl.semaphore_wait(barrier, 11)

        @pl.when(k < 3)
        def _():
            send[k] = acc[...].astype(BF)
            scatter(k).start()

        @pl.when(k == 0)
        def _():
            for d in (2, 1, 3):
                pl.semaphore_signal(plane_sem, inc=1, device_id=chip(0, d, 0), device_id_type=MESH)
            q_copy.wait()
            for n in (2, 1, 3):
                query_row(n).start()

        @pl.when(k == 1)
        def _():
            pl.semaphore_wait(plane_sem, 3)
            for d in (2, 1, 3):
                pl.semaphore_signal(all_sem, inc=1, device_id=chip(0, 0, d), device_id_type=MESH)

        @pl.when(k == 2)
        def _():
            pl.semaphore_wait(all_sem, 3)
            pltpu.make_async_copy(qbuf.at[0, 0, pl.ds(0, 3)], qbuf.at[0, 0, pl.ds(0, 3)], q_recv.at[0]).wait()

            @pl.loop(1, 8)
            def _(n):
                query_plane(n).start()

    len_copy.wait()
    seq = lax.broadcasted_iota(jnp.int32, (16, 1024), 0)
    token = lax.broadcasted_iota(jnp.int32, (16, 1024), 1) - 64 * seq
    row = seq[:, :128]
    limit = jnp.zeros((16, 128), jnp.int32)
    for s in range(16):
        limit = jnp.where(row == s, lens[zh * 16 + s], limit)
    limit = jnp.concatenate([limit] * 8, axis=1)
    live = jnp.where((token >= 0) & (token < limit), 1.0 / math.sqrt(64), 0.0).astype(BF)

    total = acc[...]
    for k in (2, 0, 1):
        scatter(k).wait_recv()
        total = total + part[k].astype(F32)
    acc[...] = total

    @pl.loop(0, 16)
    def _(a):
        prod = acc[pl.ds(16 + a, 1)] * acc[:16]
        hi, lo = split(prod)
        rows = pl.ds(pl.multiple_of(a * 16, 16), 16)
        p_hi[rows] = hi
        p_lo[rows] = lo

    own[SELF] = (nt_dot(live, p_hi[...]) + nt_dot(live, p_lo[...])).astype(BF)

    for k in range(SELF):
        pltpu.make_async_remote_copy(
            src_ref=own.at[SELF], dst_ref=own.at[k], send_sem=v_send, recv_sem=v_recv.at[k // PER_GROUP],
            device_id=chip(*OFFSETS[k]), device_id_type=MESH,
        ).start()

    def group(g):
        return pl.ds(g * PER_GROUP, PER_GROUP)

    def forward(g):
        return pltpu.make_async_remote_copy(
            src_ref=own.at[group(g)], dst_ref=oth.at[group(g)], send_sem=f_send.at[g], recv_sem=f_recv.at[g],
            device_id=sibling, device_id_type=MESH,
        )

    for g in range(GROUPS):
        got = pl.ds(g * PER_GROUP, min(PER_GROUP, SELF - g * PER_GROUP))
        pltpu.make_async_copy(own.at[got], own.at[got], v_recv.at[g]).wait()
        forward(g).start()

    gram[...] = jnp.zeros((512, 512), F32)

    @pl.loop(0, GROUPS)
    def _(g):
        forward(g).wait_recv()
        vecs = jnp.concatenate(
            [own[group(g)].reshape(256, 256), oth[group(g)].reshape(256, 256)], axis=1
        )
        gram[...] += tn_dot(vecs, vecs)

    g_hi[...] = (gram[...] * (1.0 / 1024)).astype(BF)

    rows = res.at[pl.ds(0, 448)]
    pltpu.make_async_copy(rows, rows, q_recv.at[1]).wait()
    start = jnp.concatenate(
        [qbuf[a, b, c] for a in range(4) for c in range(4) for b in range(2)], axis=0
    )
    res[...] = start
    dirn[...] = start
    sol[...] = jnp.zeros_like(start)
    norm[...] = jnp.sum(start * start, axis=0, keepdims=True)

    @pl.loop(0, ITERS)
    def _(it):
        direction = dirn[...]
        norm_now = norm[...]
        d_hi, d_lo = split(direction)
        wide = jnp.dot(g_hi[...], jnp.concatenate([d_hi, d_lo], axis=1), preferred_element_type=F32)
        image = wide[:, :128] + wide[:, 128:] + DAMPING * direction
        step_size = norm_now / jnp.sum(direction * image, axis=0, keepdims=True)
        sol[...] += step_size * direction

        @pl.when(it < ITERS - 1)
        def _():
            residual = res[...] - step_size * image
            norm_next = jnp.sum(residual * residual, axis=0, keepdims=True)
            res[...] = residual
            dirn[...] = residual + norm_next / norm_now * direction
            norm[...] = norm_next

    solution = sol[...].astype(BF)
    scale = 1.0 / math.sqrt(512)
    for slot, half in ((SELF, zh), (ACROSS, 1 - zh)):
        v = jnp.concatenate([own[slot], oth[slot]], axis=1)
        out[pl.ds(pl.multiple_of(half * 16, 16), 16)] = jnp.dot(v, solution, preferred_element_type=F32) * scale

    for k in range(3):
        scatter(k).wait_send()
    for g in range(GROUPS):
        forward(g).wait_send()
    pltpu.make_async_copy(own.at[pl.ds(0, SELF)], own.at[pl.ds(0, SELF)], v_send).wait()
    pltpu.make_async_copy(qbuf.at[0, 0, pl.ds(0, 3)], qbuf.at[0, 0, pl.ds(0, 3)], q_send.at[0]).wait()
    pltpu.make_async_copy(rows, rows, q_send.at[1]).wait()


def on_device(activations, out_grads, proj_in, proj_out, lengths, queries):
    any_space = pl.BlockSpec(memory_space=pl.ANY)
    dma = pltpu.SemaphoreType.DMA
    vmem = pltpu.VMEM
    return pl.pallas_call(
        kernel,
        out_shape=jax.ShapeDtypeStruct((32, 128), F32),
        in_specs=[any_space] * 6,
        out_specs=pl.BlockSpec(memory_space=pltpu.VMEM),
        scratch_shapes=[
            vmem((4, 1024, 1024), BF),
            vmem((4, 1024, 1024), BF),
            vmem((2, 2, 16, 1024), BF),
            vmem((3, 32, 1024), BF),
            vmem((3, 32, 1024), BF),
            vmem((32, 1024), F32),
            vmem((SLOTS, 16, 256), BF),
            vmem((SLOTS, 16, 256), BF),
            vmem((4, 2, 4, 16, 128), F32),
            pltpu.SMEM((32,), jnp.int32),
            vmem((256, 1024), BF),
            vmem((256, 1024), BF),
            vmem((512, 512), F32),
            vmem((512, 512), BF),
            vmem((512, 128), F32),
            vmem((512, 128), F32),
            vmem((512, 128), F32),
            vmem((1, 128), F32),
            dma((4, SUB, 2)),
            dma((2,)),
            dma,
            dma,
            dma((3,)),
            dma((3,)),
            dma((2,)),
            dma((2,)),
            dma,
            dma((GROUPS,)),
            dma((GROUPS,)),
            dma((GROUPS,)),
            pltpu.SemaphoreType.REGULAR,
            pltpu.SemaphoreType.REGULAR,
        ],
        compiler_params=pltpu.CompilerParams(
            collective_id=0, has_side_effects=True, vmem_limit_bytes=60 << 20
        ),
        name="influence",
    )(
        activations, out_grads, jnp.swapaxes(proj_in, 1, 2), jnp.swapaxes(proj_out, 1, 2), lengths, queries
    )


def solution(mesh):
    placed = (
        P(None, "dp", "tensor"),
        P(None, "dp", "tensor"),
        P(None, "tensor", None),
        P(None, "tensor", None),
        P("dp"),
        P("dp", "tensor"),
    )
    return jax.shard_map(
        on_device, mesh=mesh, in_specs=placed, out_specs=P("dp", "tensor"), check_vma=False
    )
```

```python
import math

import jax
import jax.numpy as jnp
from jax import lax
from jax.experimental import pallas as pl
from jax.experimental.pallas import tpu as pltpu
from jax.sharding import PartitionSpec as P

ITERS = 4
DAMPING = 0.1
MESH = pl.DeviceIdType.MESH
BF = jnp.bfloat16
F32 = jnp.float32

OFFSETS = sorted(
    [(a, b, c) for a in range(4) for b in range(4) for c in range(4)],
    key=lambda o: -sum(min(v, 4 - v) for v in o),
)
SLOTS = len(OFFSETS)
SELF = SLOTS - 1
ACROSS = OFFSETS.index((0, 0, 2))
GROUPS = 4
PER_GROUP = SLOTS // GROUPS
SUB = 2


def split(v):
    hi = v.astype(BF)
    return hi, (v - hi.astype(F32)).astype(BF)


def nt_dot(a, b):
    return lax.dot_general(a, b, (((1,), (1,)), ((), ())), preferred_element_type=F32)


def tn_dot(a, b):
    return lax.dot_general(a, b, (((0,), (0,)), ((), ())), preferred_element_type=F32)


def kernel(
    act, grad, pin, pout, lengths, queries, out,
    abuf, gbuf, pbuf, send, part, acc, own, oth, qbuf, lens, p_hi, p_lo, gram, g_hi, sol, res, dirn, norm,
    in_sem, p_sem, q_sem, l_sem, rs_send, rs_recv, q_send, q_recv, v_send, v_recv, f_send, f_recv, plane_sem, all_sem,
):
    dp, tensor = lax.axis_index("dp"), lax.axis_index("tensor")
    x, y = lax.rem(dp // 2, 4), dp // 8
    zl = lax.rem(dp, 2)
    zh, core = tensor // 2, lax.rem(tensor, 2)
    z = zh * 2 + zl

    def chip(dx, dy, dz, flip=0):
        tx, ty, tz = lax.rem(x + dx, 4), lax.rem(y + dy, 4), lax.rem(z + dz, 4)
        return ((ty * 4 + tx) * 2 + lax.rem(tz, 2), (tz // 2) * 2 + lax.rem(core + flip, 2))

    sibling = chip(0, 0, 0, 1)
    step = 1024 // SUB

    def other_linear(k):
        return lax.rem((k + 1) // 2, 2)

    def far(k):
        return 1 - k // 2

    def load(k, s, which):
        linear = lax.rem(core + other_linear(k), 2)
        half = lax.rem(zh + far(k), 2)
        src, dst = ((act, abuf), (grad, gbuf))[which]
        return pltpu.make_async_copy(
            src.at[linear, pl.ds(pl.multiple_of(half * 1024 + s * step, step), step)],
            dst.at[k, pl.ds(pl.multiple_of(s * step, step), step)],
            in_sem.at[k, s, which],
        )

    def scatter(k):
        return pltpu.make_async_remote_copy(
            src_ref=send.at[k], dst_ref=part.at[k], send_sem=rs_send.at[k], recv_sem=rs_recv.at[k],
            device_id=chip(0, 0, 2 * far(k), other_linear(k)), device_id_type=MESH,
        )

    weights = [pltpu.make_async_copy(p, pbuf.at[io], p_sem.at[io]) for io, p in enumerate((pin, pout))]
    for c in weights:
        c.start()

    @pl.loop(0, 4 * SUB)
    def _(n):
        for which in range(2):
            load(n // SUB, lax.rem(n, SUB), which).start(priority=which)

    len_copy = pltpu.make_async_copy(lengths, lens, l_sem)
    len_copy.start()
    q_y = lax.rem(y + 2 * core, 4)
    q_copy = pltpu.make_async_copy(queries, qbuf.at[q_y, zl, x], q_sem)
    q_copy.start()

    barrier = pltpu.get_barrier_semaphore()

    for t in (chip(0, 0, 2), chip(0, 0, 2, 1), sibling):
        pl.semaphore_signal(barrier, inc=1, device_id=t, device_id_type=MESH)
    for d in (1, 2, 3):
        for t in (chip(d, 0, 0), chip(0, d, 0)) + ((chip(0, 0, d),) if d != 2 else ()):
            pl.semaphore_signal(barrier, inc=1, device_id=t, device_id_type=MESH)

    def query_row(n):
        return pltpu.make_async_remote_copy(
            src_ref=qbuf.at[q_y, zl, x], dst_ref=qbuf.at[q_y, zl, x], send_sem=q_send.at[0], recv_sem=q_recv.at[0],
            device_id=chip(n, 0, 0), device_id_type=MESH,
        )

    def query_plane(n):
        ty, tl = lax.rem(y + lax.rem(n, 4), 4), lax.rem(zl + n // 4, 2)
        return pltpu.make_async_remote_copy(
            src_ref=qbuf.at[q_y, zl], dst_ref=qbuf.at[q_y, zl], send_sem=q_send.at[1], recv_sem=q_recv.at[1],
            device_id=((ty * 4 + x) * 2 + tl, tensor), device_id_type=MESH,
        )

    for c in weights:
        c.wait()

    @pl.loop(0, 4)
    def _(k):
        linear = lax.rem(core + other_linear(k), 2)

        for s in range(SUB):
            rows = pl.ds(s * step, step)
            for which, buf in enumerate((abuf, gbuf)):
                load(k, s, which).wait()
                acc[which * 16:which * 16 + 16, rows] = nt_dot(pbuf[which, linear], buf[k, rows])

        @pl.when(k == 0)
        def _():
            pl.semaphore_wait(barrier, 11)

        @pl.when(k < 3)
        def _():
            send[k] = acc[...].astype(BF)
            scatter(k).start()

        @pl.when(k == 0)
        def _():
            for d in (2, 1, 3):
                pl.semaphore_signal(plane_sem, inc=1, device_id=chip(0, d, 0), device_id_type=MESH)
            q_copy.wait()
            for n in (2, 1, 3):
                query_row(n).start()

        @pl.when(k == 1)
        def _():
            pl.semaphore_wait(plane_sem, 3)
            for d in (2, 1, 3):
                pl.semaphore_signal(all_sem, inc=1, device_id=chip(0, 0, d), device_id_type=MESH)

        @pl.when(k == 2)
        def _():
            pl.semaphore_wait(all_sem, 3)
            pltpu.make_async_copy(qbuf.at[0, 0, pl.ds(0, 3)], qbuf.at[0, 0, pl.ds(0, 3)], q_recv.at[0]).wait()

            @pl.loop(1, 8)
            def _(n):
                query_plane(n).start()

    len_copy.wait()
    seq = lax.broadcasted_iota(jnp.int32, (16, 1024), 0)
    token = lax.broadcasted_iota(jnp.int32, (16, 1024), 1) - 64 * seq
    row = seq[:, :128]
    limit = jnp.zeros((16, 128), jnp.int32)
    for s in range(16):
        limit = jnp.where(row == s, lens[zh * 16 + s], limit)
    limit = jnp.concatenate([limit] * 8, axis=1)
    live = jnp.where((token >= 0) & (token < limit), 1.0 / math.sqrt(64), 0.0).astype(BF)

    total = acc[...]
    for k in (2, 0, 1):
        scatter(k).wait_recv()
        total = total + part[k].astype(F32)
    acc[...] = total

    @pl.loop(0, 16)
    def _(a):
        prod = acc[pl.ds(16 + a, 1)] * acc[:16]
        hi, lo = split(prod)
        rows = pl.ds(pl.multiple_of(a * 16, 16), 16)
        p_hi[rows] = hi
        p_lo[rows] = lo

    own[SELF] = (nt_dot(live, p_hi[...]) + nt_dot(live, p_lo[...])).astype(BF)

    for k in range(SELF):
        pltpu.make_async_remote_copy(
            src_ref=own.at[SELF], dst_ref=own.at[k], send_sem=v_send, recv_sem=v_recv.at[k // PER_GROUP],
            device_id=chip(*OFFSETS[k]), device_id_type=MESH,
        ).start()

    def group(g):
        return pl.ds(g * PER_GROUP, PER_GROUP)

    def forward(g):
        return pltpu.make_async_remote_copy(
            src_ref=own.at[group(g)], dst_ref=oth.at[group(g)], send_sem=f_send.at[g], recv_sem=f_recv.at[g],
            device_id=sibling, device_id_type=MESH,
        )

    for g in range(GROUPS):
        got = pl.ds(g * PER_GROUP, min(PER_GROUP, SELF - g * PER_GROUP))
        pltpu.make_async_copy(own.at[got], own.at[got], v_recv.at[g]).wait()
        forward(g).start()

    gram[...] = jnp.zeros((512, 512), F32)

    @pl.loop(0, GROUPS)
    def _(g):
        forward(g).wait_recv()
        vecs = jnp.concatenate(
            [own[group(g)].reshape(256, 256), oth[group(g)].reshape(256, 256)], axis=1
        )
        gram[...] += tn_dot(vecs, vecs)

    g_hi[...] = (gram[...] * (1.0 / 1024)).astype(BF)

    rows = res.at[pl.ds(0, 448)]
    pltpu.make_async_copy(rows, rows, q_recv.at[1]).wait()
    start = jnp.concatenate(
        [qbuf[a, b, c] for a in range(4) for c in range(4) for b in range(2)], axis=0
    )
    res[...] = start
    dirn[...] = start
    sol[...] = jnp.zeros_like(start)
    norm[...] = jnp.sum(start * start, axis=0, keepdims=True)

    @pl.loop(0, ITERS)
    def _(it):
        direction = dirn[...]
        norm_now = norm[...]
        d_hi, d_lo = split(direction)
        wide = jnp.dot(g_hi[...], jnp.concatenate([d_hi, d_lo], axis=1), preferred_element_type=F32)
        image = wide[:, :128] + wide[:, 128:] + DAMPING * direction
        step_size = norm_now / jnp.sum(direction * image, axis=0, keepdims=True)
        sol[...] += step_size * direction

        @pl.when(it < ITERS - 1)
        def _():
            residual = res[...] - step_size * image
            norm_next = jnp.sum(residual * residual, axis=0, keepdims=True)
            res[...] = residual
            dirn[...] = residual + norm_next / norm_now * direction
            norm[...] = norm_next

    solution = sol[...].astype(BF)
    scale = 1.0 / math.sqrt(512)
    for slot, half in ((SELF, zh), (ACROSS, 1 - zh)):
        v = jnp.concatenate([own[slot], oth[slot]], axis=1)
        out[pl.ds(pl.multiple_of(half * 16, 16), 16)] = jnp.dot(v, solution, preferred_element_type=F32) * scale

    for k in range(3):
        scatter(k).wait_send()
    for g in range(GROUPS):
        forward(g).wait_send()
    pltpu.make_async_copy(own.at[pl.ds(0, SELF)], own.at[pl.ds(0, SELF)], v_send).wait()
    pltpu.make_async_copy(qbuf.at[0, 0, pl.ds(0, 3)], qbuf.at[0, 0, pl.ds(0, 3)], q_send.at[0]).wait()
    pltpu.make_async_copy(rows, rows, q_send.at[1]).wait()


def on_device(activations, out_grads, proj_in, proj_out, lengths, queries):
    any_space = pl.BlockSpec(memory_space=pl.ANY)
    dma = pltpu.SemaphoreType.DMA
    vmem = pltpu.VMEM
    return pl.pallas_call(
        kernel,
        out_shape=pltpu.VMEM((32, 128), F32),
        in_specs=[any_space] * 6,
        out_specs=pl.BlockSpec(memory_space=pltpu.VMEM),
        scratch_shapes=[
            vmem((4, 1024, 1024), BF),
            vmem((4, 1024, 1024), BF),
            vmem((2, 2, 16, 1024), BF),
            vmem((3, 32, 1024), BF),
            vmem((3, 32, 1024), BF),
            vmem((32, 1024), F32),
            vmem((SLOTS, 16, 256), BF),
            vmem((SLOTS, 16, 256), BF),
            vmem((4, 2, 4, 16, 128), F32),
            pltpu.SMEM((32,), jnp.int32),
            vmem((256, 1024), BF),
            vmem((256, 1024), BF),
            vmem((512, 512), F32),
            vmem((512, 512), BF),
            vmem((512, 128), F32),
            vmem((512, 128), F32),
            vmem((512, 128), F32),
            vmem((1, 128), F32),
            dma((4, SUB, 2)),
            dma((2,)),
            dma,
            dma,
            dma((3,)),
            dma((3,)),
            dma((2,)),
            dma((2,)),
            dma,
            dma((GROUPS,)),
            dma((GROUPS,)),
            dma((GROUPS,)),
            pltpu.SemaphoreType.REGULAR,
            pltpu.SemaphoreType.REGULAR,
        ],
        compiler_params=pltpu.CompilerParams(
            collective_id=0, has_side_effects=True, vmem_limit_bytes=60 << 20
        ),
        name="influence",
    )(
        activations, out_grads, jnp.swapaxes(proj_in, 1, 2), jnp.swapaxes(proj_out, 1, 2), lengths, queries
    )


def solution(mesh):
    placed = (
        P(None, "dp", "tensor"),
        P(None, "dp", "tensor"),
        P(None, "tensor", None),
        P(None, "tensor", None),
        P("dp"),
        P("dp", "tensor"),
    )
    return jax.shard_map(
        on_device, mesh=mesh, in_specs=placed, out_specs=P("dp", "tensor"), check_vma=False
    )
```

```python
import math

import jax
import jax.numpy as jnp
from jax import lax
from jax.experimental import pallas as pl
from jax.experimental.pallas import tpu as pltpu
from jax.sharding import PartitionSpec as P

ITERS = 4
DAMPING = 0.1
MESH = pl.DeviceIdType.MESH
BF = jnp.bfloat16
F32 = jnp.float32

OFFSETS = sorted(
    [(a, b, c) for a in range(4) for b in range(4) for c in range(4)],
    key=lambda o: -sum(min(v, 4 - v) for v in o),
)
SLOTS = len(OFFSETS)
SELF = SLOTS - 1
ACROSS = OFFSETS.index((0, 0, 2))
GROUPS = 4
PER_GROUP = SLOTS // GROUPS
SUB = 2


def split(v):
    hi = v.astype(BF)
    return hi, (v - hi.astype(F32)).astype(BF)


def nt_dot(a, b):
    return lax.dot_general(a, b, (((1,), (1,)), ((), ())), preferred_element_type=F32)


def tn_dot(a, b):
    return lax.dot_general(a, b, (((0,), (0,)), ((), ())), preferred_element_type=F32)


def kernel(
    act, grad, pin, pout, lengths, queries, out,
    abuf, gbuf, pbuf, send, part, acc, own, oth, qbuf, lens, p_hi, p_lo, gram, g_hi, sol, res, dirn, norm,
    in_sem, p_sem, q_sem, l_sem, rs_send, rs_recv, q_send, q_recv, v_send, v_recv, f_send, f_recv, plane_sem, all_sem,
):
    dp, tensor = lax.axis_index("dp"), lax.axis_index("tensor")
    x, y = lax.rem(dp // 2, 4), dp // 8
    zl = lax.rem(dp, 2)
    zh, core = tensor // 2, lax.rem(tensor, 2)
    z = zh * 2 + zl

    def chip(dx, dy, dz, flip=0):
        tx, ty, tz = lax.rem(x + dx, 4), lax.rem(y + dy, 4), lax.rem(z + dz, 4)
        return ((ty * 4 + tx) * 2 + lax.rem(tz, 2), (tz // 2) * 2 + lax.rem(core + flip, 2))

    sibling = chip(0, 0, 0, 1)
    step = 1024 // SUB

    def other_linear(k):
        return lax.rem((k + 1) // 2, 2)

    def far(k):
        return 1 - k // 2

    def load(k, s, which):
        linear = lax.rem(core + other_linear(k), 2)
        half = lax.rem(zh + far(k), 2)
        src, dst = ((act, abuf), (grad, gbuf))[which]
        return pltpu.make_async_copy(
            src.at[linear, pl.ds(pl.multiple_of(half * 1024 + s * step, step), step)],
            dst.at[k, pl.ds(pl.multiple_of(s * step, step), step)],
            in_sem.at[k, s, which],
        )

    def scatter(k):
        return pltpu.make_async_remote_copy(
            src_ref=send.at[k], dst_ref=part.at[k], send_sem=rs_send.at[k], recv_sem=rs_recv.at[k],
            device_id=chip(0, 0, 2 * far(k), other_linear(k)), device_id_type=MESH,
        )

    weights = [pltpu.make_async_copy(p, pbuf.at[io], p_sem.at[io]) for io, p in enumerate((pin, pout))]
    for c in weights:
        c.start()

    @pl.loop(0, 4 * SUB)
    def _(n):
        for which in range(2):
            load(n // SUB, lax.rem(n, SUB), which).start(priority=1)

    len_copy = pltpu.make_async_copy(lengths, lens, l_sem)
    len_copy.start()
    q_y = lax.rem(y + 2 * core, 4)
    q_copy = pltpu.make_async_copy(queries, qbuf.at[q_y, zl, x], q_sem)
    q_copy.start()

    barrier = pltpu.get_barrier_semaphore()

    for t in (chip(0, 0, 2), chip(0, 0, 2, 1), sibling):
        pl.semaphore_signal(barrier, inc=1, device_id=t, device_id_type=MESH)
    for d in (1, 2, 3):
        for t in (chip(d, 0, 0), chip(0, d, 0)) + ((chip(0, 0, d),) if d != 2 else ()):
            pl.semaphore_signal(barrier, inc=1, device_id=t, device_id_type=MESH)

    def query_row(n):
        return pltpu.make_async_remote_copy(
            src_ref=qbuf.at[q_y, zl, x], dst_ref=qbuf.at[q_y, zl, x], send_sem=q_send.at[0], recv_sem=q_recv.at[0],
            device_id=chip(n, 0, 0), device_id_type=MESH,
        )

    def query_plane(n):
        ty, tl = lax.rem(y + lax.rem(n, 4), 4), lax.rem(zl + n // 4, 2)
        return pltpu.make_async_remote_copy(
            src_ref=qbuf.at[q_y, zl], dst_ref=qbuf.at[q_y, zl], send_sem=q_send.at[1], recv_sem=q_recv.at[1],
            device_id=((ty * 4 + x) * 2 + tl, tensor), device_id_type=MESH,
        )

    for c in weights:
        c.wait()

    @pl.loop(0, 4)
    def _(k):
        linear = lax.rem(core + other_linear(k), 2)

        for s in range(SUB):
            rows = pl.ds(s * step, step)
            for which, buf in enumerate((abuf, gbuf)):
                load(k, s, which).wait()
                acc[which * 16:which * 16 + 16, rows] = nt_dot(pbuf[which, linear], buf[k, rows])

        @pl.when(k == 0)
        def _():
            pl.semaphore_wait(barrier, 11)

        @pl.when(k < 3)
        def _():
            send[k] = acc[...].astype(BF)
            scatter(k).start()

        @pl.when(k == 0)
        def _():
            for d in (2, 1, 3):
                pl.semaphore_signal(plane_sem, inc=1, device_id=chip(0, d, 0), device_id_type=MESH)
            q_copy.wait()
            for n in (2, 1, 3):
                query_row(n).start()

        @pl.when(k == 1)
        def _():
            pl.semaphore_wait(plane_sem, 3)
            for d in (2, 1, 3):
                pl.semaphore_signal(all_sem, inc=1, device_id=chip(0, 0, d), device_id_type=MESH)

        @pl.when(k == 2)
        def _():
            pl.semaphore_wait(all_sem, 3)
            pltpu.make_async_copy(qbuf.at[0, 0, pl.ds(0, 3)], qbuf.at[0, 0, pl.ds(0, 3)], q_recv.at[0]).wait()

            @pl.loop(1, 8)
            def _(n):
                query_plane(n).start()

    len_copy.wait()
    seq = lax.broadcasted_iota(jnp.int32, (16, 1024), 0)
    token = lax.broadcasted_iota(jnp.int32, (16, 1024), 1) - 64 * seq
    row = seq[:, :128]
    limit = jnp.zeros((16, 128), jnp.int32)
    for s in range(16):
        limit = jnp.where(row == s, lens[zh * 16 + s], limit)
    limit = jnp.concatenate([limit] * 8, axis=1)
    live = jnp.where((token >= 0) & (token < limit), 1.0 / math.sqrt(64), 0.0).astype(BF)

    total = acc[...]
    for k in (2, 0, 1):
        scatter(k).wait_recv()
        total = total + part[k].astype(F32)
    acc[...] = total

    @pl.loop(0, 16)
    def _(a):
        prod = acc[pl.ds(16 + a, 1)] * acc[:16]
        hi, lo = split(prod)
        rows = pl.ds(pl.multiple_of(a * 16, 16), 16)
        p_hi[rows] = hi
        p_lo[rows] = lo

    own[SELF] = (nt_dot(live, p_hi[...]) + nt_dot(live, p_lo[...])).astype(BF)

    for k in range(SELF):
        pltpu.make_async_remote_copy(
            src_ref=own.at[SELF], dst_ref=own.at[k], send_sem=v_send, recv_sem=v_recv.at[k // PER_GROUP],
            device_id=chip(*OFFSETS[k]), device_id_type=MESH,
        ).start()

    def group(g):
        return pl.ds(g * PER_GROUP, PER_GROUP)

    def forward(g):
        return pltpu.make_async_remote_copy(
            src_ref=own.at[group(g)], dst_ref=oth.at[group(g)], send_sem=f_send.at[g], recv_sem=f_recv.at[g],
            device_id=sibling, device_id_type=MESH,
        )

    for g in range(GROUPS):
        got = pl.ds(g * PER_GROUP, min(PER_GROUP, SELF - g * PER_GROUP))
        pltpu.make_async_copy(own.at[got], own.at[got], v_recv.at[g]).wait()
        forward(g).start()

    gram[...] = jnp.zeros((512, 512), F32)

    @pl.loop(0, GROUPS)
    def _(g):
        forward(g).wait_recv()
        vecs = jnp.concatenate(
            [own[group(g)].reshape(256, 256), oth[group(g)].reshape(256, 256)], axis=1
        )
        gram[...] += tn_dot(vecs, vecs)

    g_hi[...] = (gram[...] * (1.0 / 1024)).astype(BF)

    rows = res.at[pl.ds(0, 448)]
    pltpu.make_async_copy(rows, rows, q_recv.at[1]).wait()
    start = jnp.concatenate(
        [qbuf[a, b, c] for a in range(4) for c in range(4) for b in range(2)], axis=0
    )
    res[...] = start
    dirn[...] = start
    sol[...] = jnp.zeros_like(start)
    norm[...] = jnp.sum(start * start, axis=0, keepdims=True)

    @pl.loop(0, ITERS)
    def _(it):
        direction = dirn[...]
        norm_now = norm[...]
        d_hi, d_lo = split(direction)
        wide = jnp.dot(g_hi[...], jnp.concatenate([d_hi, d_lo], axis=1), preferred_element_type=F32)
        image = wide[:, :128] + wide[:, 128:] + DAMPING * direction
        step_size = norm_now / jnp.sum(direction * image, axis=0, keepdims=True)
        sol[...] += step_size * direction

        @pl.when(it < ITERS - 1)
        def _():
            residual = res[...] - step_size * image
            norm_next = jnp.sum(residual * residual, axis=0, keepdims=True)
            res[...] = residual
            dirn[...] = residual + norm_next / norm_now * direction
            norm[...] = norm_next

    solution = sol[...].astype(BF)
    scale = 1.0 / math.sqrt(512)
    for slot, half in ((SELF, zh), (ACROSS, 1 - zh)):
        v = jnp.concatenate([own[slot], oth[slot]], axis=1)
        out[pl.ds(pl.multiple_of(half * 16, 16), 16)] = jnp.dot(v, solution, preferred_element_type=F32) * scale

    for k in range(3):
        scatter(k).wait_send()
    for g in range(GROUPS):
        forward(g).wait_send()
    pltpu.make_async_copy(own.at[pl.ds(0, SELF)], own.at[pl.ds(0, SELF)], v_send).wait()
    pltpu.make_async_copy(qbuf.at[0, 0, pl.ds(0, 3)], qbuf.at[0, 0, pl.ds(0, 3)], q_send.at[0]).wait()
    pltpu.make_async_copy(rows, rows, q_send.at[1]).wait()


def on_device(activations, out_grads, proj_in, proj_out, lengths, queries):
    any_space = pl.BlockSpec(memory_space=pl.ANY)
    dma = pltpu.SemaphoreType.DMA
    vmem = pltpu.VMEM
    return pl.pallas_call(
        kernel,
        out_shape=pltpu.VMEM((32, 128), F32),
        in_specs=[any_space] * 6,
        out_specs=pl.BlockSpec(memory_space=pltpu.VMEM),
        scratch_shapes=[
            vmem((4, 1024, 1024), BF),
            vmem((4, 1024, 1024), BF),
            vmem((2, 2, 16, 1024), BF),
            vmem((3, 32, 1024), BF),
            vmem((3, 32, 1024), BF),
            vmem((32, 1024), F32),
            vmem((SLOTS, 16, 256), BF),
            vmem((SLOTS, 16, 256), BF),
            vmem((4, 2, 4, 16, 128), F32),
            pltpu.SMEM((32,), jnp.int32),
            vmem((256, 1024), BF),
            vmem((256, 1024), BF),
            vmem((512, 512), F32),
            vmem((512, 512), BF),
            vmem((512, 128), F32),
            vmem((512, 128), F32),
            vmem((512, 128), F32),
            vmem((1, 128), F32),
            dma((4, SUB, 2)),
            dma((2,)),
            dma,
            dma,
            dma((3,)),
            dma((3,)),
            dma((2,)),
            dma((2,)),
            dma,
            dma((GROUPS,)),
            dma((GROUPS,)),
            dma((GROUPS,)),
            pltpu.SemaphoreType.REGULAR,
            pltpu.SemaphoreType.REGULAR,
        ],
        compiler_params=pltpu.CompilerParams(
            collective_id=0, has_side_effects=True, vmem_limit_bytes=60 << 20
        ),
        name="influence",
    )(
        activations, out_grads, jnp.swapaxes(proj_in, 1, 2), jnp.swapaxes(proj_out, 1, 2), lengths, queries
    )


def solution(mesh):
    placed = (
        P(None, "dp", "tensor"),
        P(None, "dp", "tensor"),
        P(None, "tensor", None),
        P(None, "tensor", None),
        P("dp"),
        P("dp", "tensor"),
    )
    return jax.shard_map(
        on_device, mesh=mesh, in_specs=placed, out_specs=P("dp", "tensor"), check_vma=False
    )
```

```python
import math

import jax
import jax.numpy as jnp
from jax import lax
from jax.experimental import pallas as pl
from jax.experimental.pallas import tpu as pltpu
from jax.sharding import PartitionSpec as P

ITERS = 4
DAMPING = 0.1
MESH = pl.DeviceIdType.MESH
BF = jnp.bfloat16
F32 = jnp.float32

OFFSETS = sorted(
    [(a, b, c) for a in range(4) for b in range(4) for c in range(4)],
    key=lambda o: -sum(min(v, 4 - v) for v in o),
)
SLOTS = len(OFFSETS)
SELF = SLOTS - 1
ACROSS = OFFSETS.index((0, 0, 2))
GROUPS = 4
PER_GROUP = SLOTS // GROUPS
SUB = 2


def split(v):
    hi = v.astype(BF)
    return hi, (v - hi.astype(F32)).astype(BF)


def nt_dot(a, b):
    return lax.dot_general(a, b, (((1,), (1,)), ((), ())), preferred_element_type=F32)


def tn_dot(a, b):
    return lax.dot_general(a, b, (((0,), (0,)), ((), ())), preferred_element_type=F32)


def kernel(
    act, grad, pin, pout, lengths, queries, out,
    abuf, gbuf, pbuf, send, part, acc, own, oth, qbuf, lens, p_hi, p_lo, gram, g_hi, sol, res, dirn, norm,
    in_sem, p_sem, q_sem, l_sem, rs_send, rs_recv, q_send, q_recv, v_send, v_recv, f_send, f_recv, plane_sem, all_sem,
):
    dp, tensor = lax.axis_index("dp"), lax.axis_index("tensor")
    x, y = lax.rem(dp // 2, 4), dp // 8
    zl = lax.rem(dp, 2)
    zh, core = tensor // 2, lax.rem(tensor, 2)
    z = zh * 2 + zl

    def chip(dx, dy, dz, flip=0):
        tx, ty, tz = lax.rem(x + dx, 4), lax.rem(y + dy, 4), lax.rem(z + dz, 4)
        return ((ty * 4 + tx) * 2 + lax.rem(tz, 2), (tz // 2) * 2 + lax.rem(core + flip, 2))

    sibling = chip(0, 0, 0, 1)
    step = 1024 // SUB

    def other_linear(k):
        return lax.rem((k + 1) // 2, 2)

    def far(k):
        return 1 - k // 2

    def load(k, s, which):
        linear = lax.rem(core + other_linear(k), 2)
        half = lax.rem(zh + far(k), 2)
        src, dst = ((act, abuf), (grad, gbuf))[which]
        return pltpu.make_async_copy(
            src.at[linear, pl.ds(pl.multiple_of(half * 1024 + s * step, step), step)],
            dst.at[k, pl.ds(pl.multiple_of(s * step, step), step)],
            in_sem.at[k, s, which],
        )

    def scatter(k):
        return pltpu.make_async_remote_copy(
            src_ref=send.at[k], dst_ref=part.at[k], send_sem=rs_send.at[k], recv_sem=rs_recv.at[k],
            device_id=chip(0, 0, 2 * far(k), other_linear(k)), device_id_type=MESH,
        )

    weights = [pltpu.make_async_copy(p, pbuf.at[io], p_sem.at[io]) for io, p in enumerate((pin, pout))]
    for c in weights:
        c.start()

    @pl.loop(0, 4 * SUB)
    def _(n):
        for which in range(2):
            load(n // SUB, lax.rem(n, SUB), which).start(priority=1)

    len_copy = pltpu.make_async_copy(lengths, lens, l_sem)
    len_copy.start()
    q_y = lax.rem(y + 2 * core, 4)
    q_copy = pltpu.make_async_copy(queries, qbuf.at[q_y, zl, x], q_sem)
    q_copy.start()

    barrier = pltpu.get_barrier_semaphore()

    for t in (chip(0, 0, 2), chip(0, 0, 2, 1), sibling):
        pl.semaphore_signal(barrier, inc=1, device_id=t, device_id_type=MESH)
    for d in (1, 2, 3):
        for t in (chip(d, 0, 0), chip(0, d, 0)) + ((chip(0, 0, d),) if d != 2 else ()):
            pl.semaphore_signal(barrier, inc=1, device_id=t, device_id_type=MESH)

    def query_row(n):
        return pltpu.make_async_remote_copy(
            src_ref=qbuf.at[q_y, zl, x], dst_ref=qbuf.at[q_y, zl, x], send_sem=q_send.at[0], recv_sem=q_recv.at[0],
            device_id=chip(n, 0, 0), device_id_type=MESH,
        )

    def query_plane(n):
        ty, tl = lax.rem(y + lax.rem(n, 4), 4), lax.rem(zl + n // 4, 2)
        return pltpu.make_async_remote_copy(
            src_ref=qbuf.at[q_y, zl], dst_ref=qbuf.at[q_y, zl], send_sem=q_send.at[1], recv_sem=q_recv.at[1],
            device_id=((ty * 4 + x) * 2 + tl, tensor), device_id_type=MESH,
        )

    for c in weights:
        c.wait()

    @pl.loop(0, 4)
    def _(k):
        linear = lax.rem(core + other_linear(k), 2)

        for s in range(SUB):
            rows = pl.ds(s * step, step)
            for which, buf in enumerate((abuf, gbuf)):
                load(k, s, which).wait()
                acc[which * 16:which * 16 + 16, rows] = nt_dot(pbuf[which, linear], buf[k, rows])

        @pl.when(k == 0)
        def _():
            pl.semaphore_wait(barrier, 11)

        @pl.when(k < 3)
        def _():
            send[k] = acc[...].astype(BF)
            scatter(k).start()

        @pl.when(k == 0)
        def _():
            for d in (2, 1, 3):
                pl.semaphore_signal(plane_sem, inc=1, device_id=chip(0, d, 0), device_id_type=MESH)
            q_copy.wait()
            for n in (2, 1, 3):
                query_row(n).start()

        @pl.when(k == 1)
        def _():
            pl.semaphore_wait(plane_sem, 3)
            for d in (2, 1, 3):
                pl.semaphore_signal(all_sem, inc=1, device_id=chip(0, 0, d), device_id_type=MESH)

        @pl.when(k == 2)
        def _():
            pl.semaphore_wait(all_sem, 3)

    len_copy.wait()
    seq = lax.broadcasted_iota(jnp.int32, (16, 1024), 0)
    token = lax.broadcasted_iota(jnp.int32, (16, 1024), 1) - 64 * seq
    row = seq[:, :128]
    limit = jnp.zeros((16, 128), jnp.int32)
    for s in range(16):
        limit = jnp.where(row == s, lens[zh * 16 + s], limit)
    limit = jnp.concatenate([limit] * 8, axis=1)
    live = jnp.where((token >= 0) & (token < limit), 1.0 / math.sqrt(64), 0.0).astype(BF)

    total = acc[...]
    for k in (2, 0, 1):
        scatter(k).wait_recv()
        total = total + part[k].astype(F32)
    acc[...] = total

    @pl.loop(0, 16)
    def _(a):
        prod = acc[pl.ds(16 + a, 1)] * acc[:16]
        hi, lo = split(prod)
        rows = pl.ds(pl.multiple_of(a * 16, 16), 16)
        p_hi[rows] = hi
        p_lo[rows] = lo

    own[SELF] = (nt_dot(live, p_hi[...]) + nt_dot(live, p_lo[...])).astype(BF)

    for k in range(SELF):
        pltpu.make_async_remote_copy(
            src_ref=own.at[SELF], dst_ref=own.at[k], send_sem=v_send, recv_sem=v_recv.at[k // PER_GROUP],
            device_id=chip(*OFFSETS[k]), device_id_type=MESH,
        ).start()

    pltpu.make_async_copy(qbuf.at[0, 0, pl.ds(0, 3)], qbuf.at[0, 0, pl.ds(0, 3)], q_recv.at[0]).wait()

    @pl.loop(1, 8)
    def _(n):
        query_plane(n).start()

    def group(g):
        return pl.ds(g * PER_GROUP, PER_GROUP)

    def forward(g):
        return pltpu.make_async_remote_copy(
            src_ref=own.at[group(g)], dst_ref=oth.at[group(g)], send_sem=f_send.at[g], recv_sem=f_recv.at[g],
            device_id=sibling, device_id_type=MESH,
        )

    for g in range(GROUPS):
        got = pl.ds(g * PER_GROUP, min(PER_GROUP, SELF - g * PER_GROUP))
        pltpu.make_async_copy(own.at[got], own.at[got], v_recv.at[g]).wait()
        forward(g).start()

    gram[...] = jnp.zeros((512, 512), F32)

    @pl.loop(0, GROUPS)
    def _(g):
        forward(g).wait_recv()
        vecs = jnp.concatenate(
            [own[group(g)].reshape(256, 256), oth[group(g)].reshape(256, 256)], axis=1
        )
        gram[...] += tn_dot(vecs, vecs)

    g_hi[...] = (gram[...] * (1.0 / 1024)).astype(BF)

    rows = res.at[pl.ds(0, 448)]
    pltpu.make_async_copy(rows, rows, q_recv.at[1]).wait()
    start = jnp.concatenate(
        [qbuf[a, b, c] for a in range(4) for c in range(4) for b in range(2)], axis=0
    )
    res[...] = start
    dirn[...] = start
    sol[...] = jnp.zeros_like(start)
    norm[...] = jnp.sum(start * start, axis=0, keepdims=True)

    @pl.loop(0, ITERS)
    def _(it):
        direction = dirn[...]
        norm_now = norm[...]
        d_hi, d_lo = split(direction)
        wide = jnp.dot(g_hi[...], jnp.concatenate([d_hi, d_lo], axis=1), preferred_element_type=F32)
        image = wide[:, :128] + wide[:, 128:] + DAMPING * direction
        step_size = norm_now / jnp.sum(direction * image, axis=0, keepdims=True)
        sol[...] += step_size * direction

        @pl.when(it < ITERS - 1)
        def _():
            residual = res[...] - step_size * image
            norm_next = jnp.sum(residual * residual, axis=0, keepdims=True)
            res[...] = residual
            dirn[...] = residual + norm_next / norm_now * direction
            norm[...] = norm_next

    solution = sol[...].astype(BF)
    scale = 1.0 / math.sqrt(512)
    for slot, half in ((SELF, zh), (ACROSS, 1 - zh)):
        v = jnp.concatenate([own[slot], oth[slot]], axis=1)
        out[pl.ds(pl.multiple_of(half * 16, 16), 16)] = jnp.dot(v, solution, preferred_element_type=F32) * scale

    for k in range(3):
        scatter(k).wait_send()
    for g in range(GROUPS):
        forward(g).wait_send()
    pltpu.make_async_copy(own.at[pl.ds(0, SELF)], own.at[pl.ds(0, SELF)], v_send).wait()
    pltpu.make_async_copy(qbuf.at[0, 0, pl.ds(0, 3)], qbuf.at[0, 0, pl.ds(0, 3)], q_send.at[0]).wait()
    pltpu.make_async_copy(rows, rows, q_send.at[1]).wait()


def on_device(activations, out_grads, proj_in, proj_out, lengths, queries):
    any_space = pl.BlockSpec(memory_space=pl.ANY)
    dma = pltpu.SemaphoreType.DMA
    vmem = pltpu.VMEM
    return pl.pallas_call(
        kernel,
        out_shape=pltpu.VMEM((32, 128), F32),
        in_specs=[any_space] * 6,
        out_specs=pl.BlockSpec(memory_space=pltpu.VMEM),
        scratch_shapes=[
            vmem((4, 1024, 1024), BF),
            vmem((4, 1024, 1024), BF),
            vmem((2, 2, 16, 1024), BF),
            vmem((3, 32, 1024), BF),
            vmem((3, 32, 1024), BF),
            vmem((32, 1024), F32),
            vmem((SLOTS, 16, 256), BF),
            vmem((SLOTS, 16, 256), BF),
            vmem((4, 2, 4, 16, 128), F32),
            pltpu.SMEM((32,), jnp.int32),
            vmem((256, 1024), BF),
            vmem((256, 1024), BF),
            vmem((512, 512), F32),
            vmem((512, 512), BF),
            vmem((512, 128), F32),
            vmem((512, 128), F32),
            vmem((512, 128), F32),
            vmem((1, 128), F32),
            dma((4, SUB, 2)),
            dma((2,)),
            dma,
            dma,
            dma((3,)),
            dma((3,)),
            dma((2,)),
            dma((2,)),
            dma,
            dma((GROUPS,)),
            dma((GROUPS,)),
            dma((GROUPS,)),
            pltpu.SemaphoreType.REGULAR,
            pltpu.SemaphoreType.REGULAR,
        ],
        compiler_params=pltpu.CompilerParams(
            collective_id=0, has_side_effects=True, vmem_limit_bytes=60 << 20
        ),
        name="influence",
    )(
        activations, out_grads, jnp.swapaxes(proj_in, 1, 2), jnp.swapaxes(proj_out, 1, 2), lengths, queries
    )


def solution(mesh):
    placed = (
        P(None, "dp", "tensor"),
        P(None, "dp", "tensor"),
        P(None, "tensor", None),
        P(None, "tensor", None),
        P("dp"),
        P("dp", "tensor"),
    )
    return jax.shard_map(
        on_device, mesh=mesh, in_specs=placed, out_specs=P("dp", "tensor"), check_vma=False
    )
```
